32 devices in a mesh: blk: 8 (over y, x, core), exp: 4 (over z).
Axes of the slice: x: 2, y: 2, z: 4, core: 2. Of those that a mesh axis runs over, the one named last changes fastest.
Arguments:
- residual_deposit_sequence: bfloat16 [4, 1024, 1536], P('exp', 'blk'), may hold values from -60 to 60
- premix_rescaler: float32 [1536], replicated, may hold values from 0.25 to 1.75
- asking_projector: bfloat16 [1536, 1536], P(None, 'exp'), may hold values from -0.15625 to 0.15625
- lookup_projector: bfloat16 [1536, 512], P(None, 'exp'), may hold values from -0.15625 to 0.15625
- content_projector: bfloat16 [1536, 512], P(None, 'exp'), may hold values from -0.15625 to 0.15625
- final_projector: bfloat16 [1536, 1536], P('exp'), may hold values from -0.15625 to 0.15625
- logit_multipliers: float32 [12], replicated, may hold values from 1.5 to 6
- premixture_rescaler: float32 [1536], replicated, may hold values from 0.25 to 1.75
- specialist_switch_tensor: bfloat16 [8, 1536, 384], P('exp'), may hold values from -0.15625 to 0.15625
- specialist_widen_tensor: bfloat16 [8, 1536, 384], P('exp'), may hold values from -0.15625 to 0.15625
- specialist_shrink_tensor: bfloat16 [8, 384, 1536], P('exp'), may hold values from -0.3125 to 0.3125
- picked_specialist_labels: int32 [4, 1024, 2], P(None, 'blk'), may hold values from 0 to 7, all different within a row; in each aligned block of 128 rows (0 to 127, 128 to 255, ..., all dimensions but the last counted through in order) at most 64 rows name the same one
- specialist_shares: float32 [4, 1024, 2], P(None, 'blk'), may hold values from 0.1 to 1
Outputs:
- attention_update: bfloat16 [4, 1024, 1536], P('exp', 'blk')
- expert_update: bfloat16 [4, 1024, 1536], P('exp', 'blk')
The draws below stay inside these ranges and needn't reach their ends.
Inputs may be any that keep to these rules, and one draw needn't show every extreme that they name: `picked_specialist_labels`: the 2 ids of a hit differ. Within each event's 128 hits on one index of blk (an aligned block of 128 rows) no expert is named by more than 64 hits, a bound that some block reaches.
All inputs are finite; a program needn't handle non-finite values.
Results may differ from the reference program's by a relative error of at most 0.019.
Values may be sent and summed in bfloat16 or wider, within the bound.
A program may use at most 192 MiB of HBM per device.

```python
import math
import jax
import jax.numpy as jnp
import numpy as np
from jax import lax

D = 1536
ASKING_LANES = 12
LOOKUP_LANES = 4
PER_LANE_DIM = 128
FFE = 384
TOP = 2
TOK_SEQ = 128
EXPERTS = 8
LEN = 1024
SEQS = 4
CAP = 64


def draw_residual_deposit_sequence(key, part):
    key_base, key_rows, key_cols = jax.random.split(key, 3)
    samples = jnp.clip(jax.random.normal(key_base, (SEQS, LEN, D), jnp.float32), -6.0, 6.0)
    ceiling = jnp.log(10.0)
    row_scale = jnp.exp(jax.random.uniform(key_rows, (SEQS, LEN, 1), jnp.float32, 0.0, 1.0) * ceiling)
    col_scale = jnp.exp(jax.random.uniform(key_cols, (D,), jnp.float32, 0.0, 1.0) * ceiling)
    return (0.1 * samples * row_scale * col_scale).astype(jnp.bfloat16)


def steps_of(key, extent, cuts, low, high):
    def one(axis_at, shards_of):
        heights = jax.random.uniform(jax.random.fold_in(jax.random.fold_in(key, 6), axis_at), (shards_of,), jnp.float32, low / len(cuts), high / len(cuts))
        return jnp.repeat(jnp.exp(heights), extent[axis_at] // shards_of).reshape((-1,) + (1,) * (len(extent) - axis_at - 1))

    level = one(*cuts[0])
    for cut in cuts[1:]:
        level = level * one(*cut)
    return level


def deal_out(own_key, own, number, rows, number_of, top, most, slope):
    order = jax.random.permutation(own_key, number_of)
    packed, usual = load_shares(number_of, rows * top, most, slope, True), load_shares(number_of, rows * top, most, slope, False)
    places = jnp.arange(number_of)

    def named(lengths, rotation):
        used = int((lengths > 0).sum())
        fixed = max(1, used // 4)
        shifted = fixed + (places - fixed + rotation * (used - fixed)) % max(1, number_of - fixed)
        return jnp.zeros((number_of,), jnp.int32).at[order[jnp.where(places < fixed, places, shifted)]].set(jnp.asarray(lengths, jnp.int32))

    lengths = jnp.where(number % 4 == 0, named(packed, number // 4), named(usual, number - number // 4 - 1))
    mixed = jax.random.permutation(jax.random.fold_in(own, 3), number_of)
    giver, sink = mixed[0:number_of // 2 * 2:2], mixed[1:number_of // 2 * 2:2]
    slack = jnp.minimum(lengths[giver] - 1, most - lengths[sink]) // 2
    slack = jnp.where((giver == order[0]) | (sink == order[0]) | (lengths[sink] == 0), 0, jnp.maximum(slack, 0))
    shifted = jax.random.randint(jax.random.fold_in(own, 4), (number_of // 2,), 0, 1 << 20) % (slack + 1)
    lengths = lengths.at[giver].add(-shifted).at[sink].add(shifted)
    labels = jnp.searchsorted(jnp.cumsum(lengths), jnp.arange(rows * top), side="right").astype(jnp.int32)
    grid = labels.reshape(top, rows).T
    grid = grid[jax.random.permutation(jax.random.fold_in(own, 1), rows)]
    rotation = jax.random.randint(jax.random.fold_in(own, 2), (rows, 1), 0, top)
    return jnp.take_along_axis(grid, (jnp.arange(top)[None, :] + rotation) % top, axis=1)


def load_shares(amount, total, reach, lean, full):
    loads = [(1 << 20) // math.isqrt(standing ** lean) + 1 for standing in range(1, amount + 1)]
    largest = reach if full else min(reach, max(-(-total // amount), total * loads[0] // sum(loads)))
    least = 1 if total - largest >= amount - 1 else 0
    holding, spare = [largest] + [least] * (amount - 1), total - largest - least * (amount - 1)
    while spare > 0:
        movable = [i for i in range(1, amount) if holding[i] < largest] or [i for i in range(1, amount) if holding[i] < reach]
        whole, remaining = sum([loads[i] for i in movable]), spare
        for i in movable:
            extra = min(reach - holding[i], max(1, remaining * loads[i] // whole), spare)
            holding[i] = holding[i] + extra
            spare = spare - extra
    return np.array(holding)


def gaussian(own_key, shape, width, limit, cuts=(), kind=jnp.bfloat16):
    factor_of = steps_of(own_key, shape, cuts, -0.22, 0.18) if cuts else 1.0
    drawn = jax.random.normal(own_key, shape, jnp.float32) * width * factor_of
    return jnp.minimum(jnp.maximum(drawn, -limit), limit).astype(kind)


def setup_inputs(seed: int = 0) -> dict:
    key_list = jax.random.split(jax.random.key(seed), 14)
    residual_deposit_sequence = draw_residual_deposit_sequence(jax.random.fold_in(key_list[13], 71), 0)
    premix_rescaler = jnp.clip(1.0 + 0.15 * jax.random.normal(key_list[1], (D,), jnp.float32), 0.25, 1.75)
    asking_projector = gaussian(key_list[2], (D, ASKING_LANES * PER_LANE_DIM), D ** -0.5, 0.15625, ((1, 4),))
    lookup_projector = gaussian(key_list[3], (D, LOOKUP_LANES * PER_LANE_DIM), D ** -0.5, 0.15625, ((1, 4),))
    content_projector = gaussian(key_list[4], (D, LOOKUP_LANES * PER_LANE_DIM), D ** -0.5, 0.15625, ((1, 4),))
    final_projector = gaussian(key_list[5], (ASKING_LANES * PER_LANE_DIM, D), (ASKING_LANES * PER_LANE_DIM) ** -0.5, 0.15625, ((0, 4),))
    logit_multipliers = jnp.clip(jnp.exp(jax.random.uniform(key_list[6], (ASKING_LANES,), jnp.float32, math.log(1.5), math.log(6.0))), 1.5, 6.0)
    premixture_rescaler = jnp.clip(1.0 + 0.15 * jax.random.normal(key_list[7], (D,), jnp.float32), 0.25, 1.75)
    specialist_switch_tensor = gaussian(key_list[8], (EXPERTS, D, FFE), D ** -0.5, 0.15625, ((0, 4),))
    specialist_widen_tensor = gaussian(key_list[9], (EXPERTS, D, FFE), D ** -0.5, 0.15625, ((0, 4),))
    specialist_shrink_tensor = gaussian(key_list[10], (EXPERTS, FFE, D), FFE ** -0.5, 0.3125, ((0, 4),))
    picked_specialist_labels_keys = jax.random.split(jax.random.fold_in(key_list[11], 1), SEQS * LEN // TOK_SEQ)
    picked_specialist_labels_turns = jax.random.permutation(jax.random.fold_in(key_list[11], 3), SEQS * LEN // TOK_SEQ)
    picked_specialist_labels = jax.vmap(lambda own, number: deal_out(jax.random.fold_in(key_list[11], 2), own, number, TOK_SEQ, EXPERTS, TOP, CAP, 2))(picked_specialist_labels_keys, picked_specialist_labels_turns).reshape((SEQS, LEN, TOP))
    specialist_shares = jnp.clip(0.1 + 0.9 * jax.random.uniform(key_list[12], (SEQS, LEN, TOP), jnp.float32) ** steps_of(key_list[12], (SEQS, LEN, TOP), ((1, 8),), -0.2, 0.2), 0.1, 1.0)
    return dict(residual_deposit_sequence=residual_deposit_sequence, premix_rescaler=premix_rescaler, asking_projector=asking_projector, lookup_projector=lookup_projector, content_projector=content_projector, final_projector=final_projector, logit_multipliers=logit_multipliers, premixture_rescaler=premixture_rescaler, specialist_switch_tensor=specialist_switch_tensor, specialist_widen_tensor=specialist_widen_tensor, specialist_shrink_tensor=specialist_shrink_tensor, picked_specialist_labels=picked_specialist_labels, specialist_shares=specialist_shares)


def rounded(values):
    return lax.optimization_barrier(values.astype(jnp.bfloat16))

def norm_rows(values, norm_gain):
    widened = values.astype(jnp.float32)
    return widened * lax.rsqrt(lax.optimization_barrier(jnp.mean(widened * widened, axis=-1, keepdims=True)) + 1e-05) * norm_gain

def head_norm(values):
    return values * lax.rsqrt(lax.optimization_barrier(jnp.mean(values * values, axis=-1, keepdims=True)) + 1e-06)

def reference(residual_deposit_sequence, premix_rescaler, asking_projector, lookup_projector, content_projector, final_projector, logit_multipliers, premixture_rescaler, specialist_switch_tensor, specialist_widen_tensor, specialist_shrink_tensor, picked_specialist_labels, specialist_shares):
    askers_per_lookup = ASKING_LANES // LOOKUP_LANES
    rescaled_entries = norm_rows(residual_deposit_sequence, premix_rescaler).astype(jnp.bfloat16)
    inverse_root_dim = (logit_multipliers / math.sqrt(PER_LANE_DIM)).reshape(LOOKUP_LANES, askers_per_lookup)
    out_wide = final_projector.astype(jnp.float32).reshape(LOOKUP_LANES, askers_per_lookup, PER_LANE_DIM, D)
    block_rows = math.gcd(LEN, 512)

    def one_event(event_rows):
        query_heads = rounded(head_norm(jnp.dot(event_rows, asking_projector, preferred_element_type=jnp.float32).reshape(LEN, LOOKUP_LANES, askers_per_lookup, PER_LANE_DIM)))
        key_heads = rounded(head_norm(jnp.dot(event_rows, lookup_projector, preferred_element_type=jnp.float32).reshape(LEN, LOOKUP_LANES, PER_LANE_DIM)))
        value_heads = rounded(jnp.dot(event_rows, content_projector, preferred_element_type=jnp.float32).reshape(LEN, LOOKUP_LANES, PER_LANE_DIM))
        key_wide = key_heads.astype(jnp.float32)
        value_wide = value_heads.astype(jnp.float32)
        blocks = query_heads.reshape(LEN // block_rows, block_rows, LOOKUP_LANES, askers_per_lookup, PER_LANE_DIM)

        def one_block(query_block):
            scores = jnp.einsum('ikgd,jkd->kgij', query_block.astype(jnp.float32), key_wide) * inverse_root_dim[:, :, None, None]
            expo = jnp.exp(scores)
            totals = lax.optimization_barrier(jnp.sum(expo, axis=-1))
            probs = rounded(expo).astype(jnp.float32)
            mixture = jnp.einsum('kgij,jkd->kgid', probs, value_wide) / totals[..., None]
            heads_out = rounded(head_norm(mixture)).astype(jnp.float32)
            return jnp.einsum('kgid,kgde->ie', heads_out, out_wide)
        return lax.map(one_block, blocks).reshape(LEN, D)
    attention_full = lax.map(one_event, rescaled_entries)
    attention_update = attention_full.astype(jnp.bfloat16)
    residual = residual_deposit_sequence.astype(jnp.float32) + attention_full
    expert_in = norm_rows(residual, premixture_rescaler).astype(jnp.bfloat16).reshape(SEQS * LEN, D)
    flat_ids = picked_specialist_labels.reshape(SEQS * LEN, TOP)
    flat_gates = specialist_shares.reshape(SEQS * LEN, TOP)

    def add_expert(running, expert_index):
        gate_act = jnp.dot(expert_in, specialist_switch_tensor[expert_index], preferred_element_type=jnp.float32)
        up_act = jnp.dot(expert_in, specialist_widen_tensor[expert_index], preferred_element_type=jnp.float32)
        hidden = (jax.nn.silu(gate_act) * up_act).astype(jnp.bfloat16)
        produced = rounded(jnp.dot(hidden, specialist_shrink_tensor[expert_index], preferred_element_type=jnp.float32)).astype(jnp.float32)
        gate_share = lax.optimization_barrier(jnp.sum(jnp.where(flat_ids == expert_index, flat_gates, 0.0), axis=1))
        return (running + gate_share[:, None] * produced, None)
    start_sum = jnp.zeros((SEQS * LEN, D), jnp.float32)
    expert_sum, unused = lax.scan(add_expert, start_sum, jnp.arange(EXPERTS, dtype=jnp.int32))
    expert_update = expert_sum.astype(jnp.bfloat16).reshape(SEQS, LEN, D)
    return (attention_update, expert_update)
```

```python
import math

import jax
import jax.numpy as jnp
from jax import lax
from jax.sharding import PartitionSpec as P

D = 1536
PER_LANE_DIM = 128
TOP = 2
CAP = 64


def norm_rows(values, norm_gain):
    widened = values.astype(jnp.float32)
    return (
        widened * lax.rsqrt(jnp.mean(widened * widened, axis=-1, keepdims=True) + 1e-05) * norm_gain
    )


def head_norm(values):
    return values * lax.rsqrt(jnp.mean(values * values, axis=-1, keepdims=True) + 1e-06)


def attend_hits(
    rescaled_entries,
    asking_projector,
    lookup_projector,
    content_projector,
    final_projector,
    logit_multipliers,
):
    events, row_count, model_width = rescaled_entries.shape
    common_key_heads = lookup_projector.shape[1] // PER_LANE_DIM
    local_lane_count = asking_projector.shape[1] // PER_LANE_DIM
    askers_per_lookup = local_lane_count // common_key_heads
    query_heads = jnp.einsum(
        "std,de->ste", rescaled_entries, asking_projector, preferred_element_type=jnp.float32
    )
    query_heads = head_norm(
        query_heads.reshape(events, row_count, common_key_heads, askers_per_lookup, PER_LANE_DIM)
    ).astype(jnp.bfloat16)
    key_heads = jnp.einsum(
        "std,de->ste", rescaled_entries, lookup_projector, preferred_element_type=jnp.float32
    )
    key_heads = head_norm(
        key_heads.reshape(events, row_count, common_key_heads, PER_LANE_DIM)
    ).astype(jnp.bfloat16)
    value_heads = jnp.einsum(
        "std,de->ste", rescaled_entries, content_projector, preferred_element_type=jnp.float32
    )
    value_heads = value_heads.reshape(events, row_count, common_key_heads, PER_LANE_DIM).astype(
        jnp.bfloat16
    )
    inverse_root_dim = (logit_multipliers / math.sqrt(PER_LANE_DIM)).reshape(
        common_key_heads, askers_per_lookup
    )
    key_piece = lax.all_gather(key_heads, "blk", axis=1, tiled=True)
    value_piece = lax.all_gather(value_heads, "blk", axis=1, tiled=True)
    scores = jnp.einsum(
        "sikgd,sjkd->skgij", query_heads, key_piece, preferred_element_type=jnp.float32
    )
    expo = jnp.exp(scores * inverse_root_dim[None, :, :, None, None])
    totals = jnp.sum(expo, axis=-1)
    mixture = jnp.einsum(
        "skgij,sjkd->skgid",
        expo.astype(jnp.bfloat16),
        value_piece,
        preferred_element_type=jnp.float32,
    )
    totals, mixture = (totals, mixture)
    heads_out = head_norm(mixture / totals[..., None]).astype(jnp.bfloat16)
    out_blocks = final_projector.reshape(
        common_key_heads, askers_per_lookup, PER_LANE_DIM, model_width
    )
    return jnp.einsum("skgid,kgde->sie", heads_out, out_blocks, preferred_element_type=jnp.float32)


def gates_of(labels, shares, expert_ids):
    hit = labels[..., None, :] == expert_ids[:, None]
    return jnp.sum(jnp.where(hit, shares[..., None, :], 0.0), axis=-1)


def run_experts(rows, gates, switch, widen, shrink):
    gate_act = jnp.einsum("td,jdf->tjf", rows, switch, preferred_element_type=jnp.float32)
    up_act = jnp.einsum("td,jdf->tjf", rows, widen, preferred_element_type=jnp.float32)
    hidden = (jax.nn.silu(gate_act) * up_act * gates[:, :, None]).astype(jnp.bfloat16)
    return jnp.einsum("tjf,jfd->td", hidden, shrink, preferred_element_type=jnp.float32)


def body(
    residual_deposit_sequence,
    premix_rescaler,
    asking_projector,
    lookup_projector,
    content_projector,
    final_projector,
    logit_multipliers,
    premixture_rescaler,
    specialist_switch_tensor,
    specialist_widen_tensor,
    specialist_shrink_tensor,
    picked_specialist_labels,
    specialist_shares,
):
    specialist_slot = lax.axis_index("exp")
    exp_count = lax.axis_size("exp")
    rows_all = lax.all_gather(residual_deposit_sequence, "exp", axis=0, tiled=True)
    rescaled_entries = norm_rows(rows_all, premix_rescaler).astype(jnp.bfloat16)
    local_lane_count = asking_projector.shape[1] // PER_LANE_DIM
    device_scratch = lax.dynamic_slice_in_dim(
        logit_multipliers, specialist_slot * local_lane_count, local_lane_count
    )
    partial_out = attend_hits(
        rescaled_entries,
        asking_projector,
        lookup_projector,
        content_projector,
        final_projector,
        device_scratch,
    )
    attention_full = lax.psum_scatter(
        partial_out.astype(jnp.bfloat16), "exp", scatter_dimension=0, tiled=True
    ).astype(jnp.float32)
    attention_update = attention_full.astype(jnp.bfloat16)
    residual = residual_deposit_sequence.astype(jnp.float32) + attention_full
    expert_in = norm_rows(residual, premixture_rescaler).astype(jnp.bfloat16)
    local_experts = specialist_switch_tensor.shape[0]
    expert_ids = specialist_slot * local_experts + jnp.arange(local_experts, dtype=jnp.int32)
    gates = gates_of(picked_specialist_labels, specialist_shares, expert_ids)
    rows = lax.all_gather(expert_in, "exp", axis=0, tiled=True)
    events, row_count, _ = rows.shape
    summed = run_experts(
        rows.reshape(events * row_count, D),
        gates.reshape(events * row_count, local_experts),
        specialist_switch_tensor,
        specialist_widen_tensor,
        specialist_shrink_tensor,
    ).astype(jnp.bfloat16)
    expert_update = lax.psum_scatter(
        summed.reshape(events, row_count, D), "exp", scatter_dimension=0, tiled=True
    )
    return (attention_update, expert_update)


def solution(mesh):
    placed = (
        P("exp", "blk", None),
        P(),
        P(None, "exp"),
        P(None, "exp"),
        P(None, "exp"),
        P("exp", None),
        P(),
        P(),
        P("exp", None, None),
        P("exp", None, None),
        P("exp", None, None),
        P(None, "blk", None),
        P(None, "blk", None),
    )
    return jax.shard_map(
        body,
        mesh=mesh,
        in_specs=placed,
        out_specs=(P("exp", "blk", None), P("exp", "blk", None)),
        check_vma=False,
    )
```

```python
import functools
import math

import jax
import jax.numpy as jnp
from jax import lax
from jax.experimental import pallas as pl
from jax.experimental.pallas import tpu as pltpu
from jax.sharding import PartitionSpec as P

D = 1536
PER_LANE_DIM = 128
TOP = 2
CAP = 64


def norm_rows(values, norm_gain):
    widened = values.astype(jnp.float32)
    return (
        widened * lax.rsqrt(jnp.mean(widened * widened, axis=-1, keepdims=True) + 1e-05) * norm_gain
    )


def head_norm(values):
    return values * lax.rsqrt(jnp.mean(values * values, axis=-1, keepdims=True) + 1e-06)


def attend_hits(
    rescaled_entries,
    asking_projector,
    lookup_projector,
    content_projector,
    final_projector,
    logit_multipliers,
):
    events, row_count, model_width = rescaled_entries.shape
    common_key_heads = lookup_projector.shape[1] // PER_LANE_DIM
    local_lane_count = asking_projector.shape[1] // PER_LANE_DIM
    askers_per_lookup = local_lane_count // common_key_heads
    query_heads = jnp.einsum(
        "std,de->ste", rescaled_entries, asking_projector, preferred_element_type=jnp.float32
    )
    query_heads = head_norm(
        query_heads.reshape(events, row_count, common_key_heads, askers_per_lookup, PER_LANE_DIM)
    ).astype(jnp.bfloat16)
    key_heads = jnp.einsum(
        "std,de->ste", rescaled_entries, lookup_projector, preferred_element_type=jnp.float32
    )
    key_heads = head_norm(
        key_heads.reshape(events, row_count, common_key_heads, PER_LANE_DIM)
    ).astype(jnp.bfloat16)
    value_heads = jnp.einsum(
        "std,de->ste", rescaled_entries, content_projector, preferred_element_type=jnp.float32
    )
    value_heads = value_heads.reshape(events, row_count, common_key_heads, PER_LANE_DIM).astype(
        jnp.bfloat16
    )
    inverse_root_dim = (logit_multipliers / math.sqrt(PER_LANE_DIM)).reshape(
        common_key_heads, askers_per_lookup
    )
    pair = lax.all_gather(
        jnp.concatenate([key_heads, value_heads], axis=-1), "blk", axis=1, tiled=True
    )
    key_piece, value_piece = pair[..., :PER_LANE_DIM], pair[..., PER_LANE_DIM:]
    scores = jnp.einsum(
        "sikgd,sjkd->skgij", query_heads, key_piece, preferred_element_type=jnp.float32
    )
    expo = jnp.exp(scores * inverse_root_dim[None, :, :, None, None])
    totals = jnp.sum(expo, axis=-1)
    mixture = jnp.einsum(
        "skgij,sjkd->skgid",
        expo.astype(jnp.bfloat16),
        value_piece,
        preferred_element_type=jnp.float32,
    )
    totals, mixture = (totals, mixture)
    heads_out = head_norm(mixture / totals[..., None]).astype(jnp.bfloat16)
    out_blocks = final_projector.reshape(
        common_key_heads, askers_per_lookup, PER_LANE_DIM, model_width
    )
    return jnp.einsum("skgid,kgde->sie", heads_out, out_blocks, preferred_element_type=jnp.float32)


def gates_of(labels, shares, expert_ids):
    hit = labels[..., None, :] == expert_ids[:, None]
    return jnp.sum(jnp.where(hit, shares[..., None, :], 0.0), axis=-1)


def greet_all(n, axis):
    me = lax.axis_index(axis)
    barrier = pltpu.get_barrier_semaphore()

    @pl.loop(1, n)
    def _(k):
        pl.semaphore_signal(
            barrier,
            inc=1,
            device_id={axis: lax.rem(me + k, n)},
            device_id_type=pl.DeviceIdType.MESH,
        )

    pl.semaphore_wait(barrier, n - 1)


def copy_to(src, dst, send_sem, recv_sem, **where):
    return pltpu.make_async_remote_copy(
        src_ref=src,
        dst_ref=dst,
        send_sem=send_sem,
        recv_sem=recv_sem,
        device_id=where,
        device_id_type=pl.DeviceIdType.MESH,
    )


def line_sends(n, me, s, block, held, up_sem, down_sem, recv_sem):
    up = copy_to(block, held.at[s], up_sem.at[s], recv_sem.at[s], exp=lax.rem(me + 1, n))
    down = copy_to(block, held.at[s], down_sem.at[s], recv_sem.at[s], exp=lax.rem(me + n - 1, n))
    return up, down


def experts_kernel(
    n, x_ref, gates_ref, switch, widen, shrink, out_ref,
    held, parts, back, total, up_sem, down_sem, recv_sem, ret_sem, back_sem,
):
    me = lax.axis_index("exp")
    greet_all(n, "exp")

    def sends(s, block):
        return line_sends(n, me, s, block, held, up_sem, down_sem, recv_sem)

    def expert_sum(rows, gates):
        summed = None
        for j in range(switch.shape[0]):
            gate = jnp.dot(rows, switch[j], preferred_element_type=jnp.float32)
            up = jnp.dot(rows, widen[j], preferred_element_type=jnp.float32)
            hidden = gate / (1.0 + jnp.exp(-gate)) * up * gates[:, j : j + 1]
            term = jnp.dot(
                hidden.astype(jnp.bfloat16), shrink[j], preferred_element_type=jnp.float32
            )
            summed = term if summed is None else summed + term
        return summed

    up, down = sends(me, x_ref)
    pl.when(me < n - 1)(up.start)
    pl.when(me > 0)(down.start)
    total[...] = expert_sum(x_ref[...], gates_ref[me])

    @pl.loop(1, n)
    def _(k):
        low, high = me - k, me + k

        @pl.when(low >= 0)
        def _():
            up, _ = sends(low, held.at[low])
            up.wait_recv()
            pl.when(me < n - 1)(up.start)

        @pl.when(high < n)
        def _():
            _, down = sends(high, held.at[high])
            down.wait_recv()
            pl.when(me > 0)(down.start)

        @pl.loop(0, 2)
        def _(side):
            s = me + (2 * side - 1) * k

            @pl.when((s >= 0) & (s < n))
            def _():
                parts[s] = expert_sum(held[s], gates_ref[s]).astype(jnp.bfloat16)
                copy_to(
                    parts.at[s], back.at[me], ret_sem.at[s], back_sem.at[me], exp=s
                ).start()

    @pl.loop(1, n)
    def _(k):
        f = lax.rem(me + k, n)
        copy_to(parts.at[f], back.at[f], ret_sem.at[f], back_sem.at[f], exp=f).wait_recv()
        total[...] += back[f].astype(jnp.float32)

    out_ref[...] = total[...].astype(out_ref.dtype)

    @pl.loop(1, n)
    def _(k):
        f = lax.rem(me + k, n)
        copy_to(parts.at[f], back.at[f], ret_sem.at[f], back_sem.at[f], exp=f).wait_send()

    @pl.loop(0, n)
    def _(s):
        up, down = sends(s, held.at[s])
        pl.when((s <= me) & (me < n - 1))(up.wait_send)
        pl.when((s >= me) & (me > 0))(down.wait_send)


def run_experts(expert_in, gates, switch, widen, shrink):
    n = lax.axis_size("exp")
    rows, width = expert_in.shape
    vmem = pl.BlockSpec(memory_space=pltpu.VMEM)
    return pl.pallas_call(
        functools.partial(experts_kernel, n),
        out_shape=jax.ShapeDtypeStruct((rows, width), jnp.bfloat16),
        in_specs=[vmem] * 5,
        out_specs=vmem,
        scratch_shapes=[
            pltpu.VMEM((n, rows, width), jnp.bfloat16),
            pltpu.VMEM((n, rows, width), jnp.bfloat16),
            pltpu.VMEM((n, rows, width), jnp.bfloat16),
            pltpu.VMEM((rows, width), jnp.float32),
        ]
        + [pltpu.SemaphoreType.DMA((n,))] * 5,
        compiler_params=pltpu.CompilerParams(
            collective_id=2, has_side_effects=True, vmem_limit_bytes=40 * 2**20
        ),
    )(expert_in, gates, switch, widen, shrink)


def body(
    residual_deposit_sequence,
    premix_rescaler,
    asking_projector,
    lookup_projector,
    content_projector,
    final_projector,
    logit_multipliers,
    premixture_rescaler,
    specialist_switch_tensor,
    specialist_widen_tensor,
    specialist_shrink_tensor,
    picked_specialist_labels,
    specialist_shares,
):
    specialist_slot = lax.axis_index("exp")
    exp_count = lax.axis_size("exp")
    rows_all = lax.all_gather(residual_deposit_sequence, "exp", axis=0, tiled=True)
    rescaled_entries = norm_rows(rows_all, premix_rescaler).astype(jnp.bfloat16)
    local_lane_count = asking_projector.shape[1] // PER_LANE_DIM
    device_scratch = lax.dynamic_slice_in_dim(
        logit_multipliers, specialist_slot * local_lane_count, local_lane_count
    )
    partial_out = attend_hits(
        rescaled_entries,
        asking_projector,
        lookup_projector,
        content_projector,
        final_projector,
        device_scratch,
    )
    attention_full = lax.psum_scatter(
        partial_out.astype(jnp.bfloat16), "exp", scatter_dimension=0, tiled=True
    ).astype(jnp.float32)
    attention_update = attention_full.astype(jnp.bfloat16)
    residual = residual_deposit_sequence.astype(jnp.float32) + attention_full
    expert_in = norm_rows(residual, premixture_rescaler).astype(jnp.bfloat16)
    local_experts = specialist_switch_tensor.shape[0]
    expert_ids = specialist_slot * local_experts + jnp.arange(local_experts, dtype=jnp.int32)
    gates = gates_of(picked_specialist_labels, specialist_shares, expert_ids)
    expert_update = run_experts(
        expert_in[0],
        gates,
        specialist_switch_tensor,
        specialist_widen_tensor,
        specialist_shrink_tensor,
    )[None]
    return (attention_update, expert_update)


def solution(mesh):
    placed = (
        P("exp", "blk", None),
        P(),
        P(None, "exp"),
        P(None, "exp"),
        P(None, "exp"),
        P("exp", None),
        P(),
        P(),
        P("exp", None, None),
        P("exp", None, None),
        P("exp", None, None),
        P(None, "blk", None),
        P(None, "blk", None),
    )
    return jax.shard_map(
        body,
        mesh=mesh,
        in_specs=placed,
        out_specs=(P("exp", "blk", None), P("exp", "blk", None)),
        check_vma=False,
    )
```

```python
import functools
import math

import jax
import jax.numpy as jnp
from jax import lax
from jax.experimental import pallas as pl
from jax.experimental.pallas import tpu as pltpu
from jax.sharding import PartitionSpec as P

D = 1536
PER_LANE_DIM = 128
TOP = 2
CAP = 64


def norm_rows(values, norm_gain):
    widened = values.astype(jnp.float32)
    return (
        widened * lax.rsqrt(jnp.mean(widened * widened, axis=-1, keepdims=True) + 1e-05) * norm_gain
    )


def head_norm(values):
    return values * lax.rsqrt(jnp.mean(values * values, axis=-1, keepdims=True) + 1e-06)


def attend_hits(query_heads, pairs, final_projector, logit_multipliers):
    events, row_count, _ = query_heads.shape
    lanes = logit_multipliers.shape[0]
    query_heads = query_heads.reshape(events, row_count, lanes, PER_LANE_DIM)
    pairs = jnp.swapaxes(pairs, 0, 1).reshape(events, -1, 2 * PER_LANE_DIM)
    keys, values = pairs[..., :PER_LANE_DIM], pairs[..., PER_LANE_DIM:]
    scale = logit_multipliers / math.sqrt(PER_LANE_DIM)
    scores = jnp.einsum("sigd,sjd->sgij", query_heads, keys, preferred_element_type=jnp.float32)
    expo = jnp.exp(scores * scale[None, :, None, None])
    totals = jnp.sum(expo, axis=-1)
    mixture = jnp.einsum(
        "sgij,sjd->sgid", expo.astype(jnp.bfloat16), values, preferred_element_type=jnp.float32
    )
    heads_out = head_norm(mixture / totals[..., None]).astype(jnp.bfloat16)
    out_blocks = final_projector.reshape(lanes, PER_LANE_DIM, final_projector.shape[1])
    return jnp.einsum("sgid,gde->sie", heads_out, out_blocks, preferred_element_type=jnp.float32)


def gates_of(labels, shares, expert_ids):
    hit = labels[..., None, :] == expert_ids[:, None]
    return jnp.sum(jnp.where(hit, shares[..., None, :], 0.0), axis=-1)


def greet_all(n, axis):
    me = lax.axis_index(axis)
    barrier = pltpu.get_barrier_semaphore()

    @pl.loop(1, n)
    def _(k):
        pl.semaphore_signal(
            barrier,
            inc=1,
            device_id={axis: lax.rem(me + k, n)},
            device_id_type=pl.DeviceIdType.MESH,
        )

    pl.semaphore_wait(barrier, n - 1)


def copy_to(src, dst, send_sem, recv_sem, **where):
    return pltpu.make_async_remote_copy(
        src_ref=src,
        dst_ref=dst,
        send_sem=send_sem,
        recv_sem=recv_sem,
        device_id=where,
        device_id_type=pl.DeviceIdType.MESH,
    )


def line_sends(n, me, s, block, held, up_sem, down_sem, recv_sem):
    up = copy_to(block, held.at[s], up_sem.at[s], recv_sem.at[s], exp=lax.rem(me + 1, n))
    down = copy_to(block, held.at[s], down_sem.at[s], recv_sem.at[s], exp=lax.rem(me + n - 1, n))
    return up, down


def greet_both(n, blk_count):
    me, here = lax.axis_index("exp"), lax.axis_index("blk")
    barrier = pltpu.get_barrier_semaphore()

    @pl.loop(1, n)
    def _(k):
        pl.semaphore_signal(
            barrier,
            inc=1,
            device_id={"exp": lax.rem(me + k, n)},
            device_id_type=pl.DeviceIdType.MESH,
        )

    @pl.loop(1, blk_count)
    def _(k):
        pl.semaphore_signal(
            barrier,
            inc=1,
            device_id={"blk": lax.rem(here + k, blk_count)},
            device_id_type=pl.DeviceIdType.MESH,
        )

    pl.semaphore_wait(barrier, n + blk_count - 2)


def project_kernel(
    n, blk_count, x_ref, gain, asking, lookup, content, q_ref, kv_ref,
    held, up_sem, down_sem, recv_sem, kv_send_sem, kv_recv_sem,
):
    me, here = lax.axis_index("exp"), lax.axis_index("blk")
    greet_both(n, blk_count)

    def sends(s, block):
        return line_sends(n, me, s, block, held, up_sem, down_sem, recv_sem)

    def kv_copy(s, owner, peer):
        block = kv_ref.at[owner, s]
        return copy_to(block, block, kv_send_sem.at[s, peer], kv_recv_sem.at[s, owner], blk=peer)

    def project(s, block):
        rows = norm_rows(block, gain[...]).astype(jnp.bfloat16)
        keys = jnp.dot(rows, lookup[...], preferred_element_type=jnp.float32)
        kv_ref[here, s, :, :PER_LANE_DIM] = head_norm(keys).astype(jnp.bfloat16)
        values = jnp.dot(rows, content[...], preferred_element_type=jnp.float32)
        kv_ref[here, s, :, PER_LANE_DIM:] = values.astype(jnp.bfloat16)

        @pl.loop(1, blk_count)
        def _(k):
            kv_copy(s, here, lax.rem(here + k, blk_count)).start()

        queries = jnp.dot(rows, asking[...], preferred_element_type=jnp.float32)
        for h in range(asking.shape[1] // PER_LANE_DIM):
            lane = slice(h * PER_LANE_DIM, (h + 1) * PER_LANE_DIM)
            q_ref[s, :, lane] = head_norm(queries[:, lane]).astype(jnp.bfloat16)

    up, down = sends(me, x_ref)
    pl.when(me < n - 1)(up.start)
    pl.when(me > 0)(down.start)
    project(me, x_ref[...])

    @pl.loop(1, n)
    def _(k):
        low, high = me - k, me + k

        @pl.when(low >= 0)
        def _():
            up, _ = sends(low, held.at[low])
            up.wait_recv()
            pl.when(me < n - 1)(up.start)

        @pl.when(high < n)
        def _():
            _, down = sends(high, held.at[high])
            down.wait_recv()
            pl.when(me > 0)(down.start)

        @pl.loop(0, 2)
        def _(side):
            s = me + (2 * side - 1) * k

            @pl.when((s >= 0) & (s < n))
            def _():
                project(s, held[s])

    @pl.loop(0, n)
    def _(s):
        up, down = sends(s, held.at[s])
        pl.when((s <= me) & (me < n - 1))(up.wait_send)
        pl.when((s >= me) & (me > 0))(down.wait_send)

        @pl.loop(1, blk_count)
        def _(k):
            peer = lax.rem(here + k, blk_count)
            kv_copy(s, here, peer).wait_send()
            kv_copy(s, peer, peer).wait_recv()


def project_hits(rows, gain, asking, lookup, content):
    n, blk_count = lax.axis_size("exp"), lax.axis_size("blk")
    count, width = rows.shape
    vmem = pl.BlockSpec(memory_space=pltpu.VMEM)
    return pl.pallas_call(
        functools.partial(project_kernel, n, blk_count),
        out_shape=(
            jax.ShapeDtypeStruct((n, count, asking.shape[1]), jnp.bfloat16),
            jax.ShapeDtypeStruct((blk_count, n, count, 2 * PER_LANE_DIM), jnp.bfloat16),
        ),
        in_specs=[vmem] * 5,
        out_specs=(vmem, vmem),
        scratch_shapes=[pltpu.VMEM((n, count, width), jnp.bfloat16)]
        + [pltpu.SemaphoreType.DMA((n,))] * 3
        + [pltpu.SemaphoreType.DMA((n, blk_count))] * 2,
        compiler_params=pltpu.CompilerParams(
            collective_id=1, has_side_effects=True, vmem_limit_bytes=40 * 2**20
        ),
    )(rows, gain[None], asking, lookup, content)


def experts_kernel(
    n, x_ref, gates_ref, switch, widen, shrink, out_ref,
    held, parts, back, total, up_sem, down_sem, recv_sem, ret_sem, back_sem,
):
    me = lax.axis_index("exp")
    greet_all(n, "exp")

    def sends(s, block):
        return line_sends(n, me, s, block, held, up_sem, down_sem, recv_sem)

    def expert_sum(rows, gates):
        summed = None
        for j in range(switch.shape[0]):
            gate = jnp.dot(rows, switch[j], preferred_element_type=jnp.float32)
            up = jnp.dot(rows, widen[j], preferred_element_type=jnp.float32)
            hidden = gate / (1.0 + jnp.exp(-gate)) * up * gates[:, j : j + 1]
            term = jnp.dot(
                hidden.astype(jnp.bfloat16), shrink[j], preferred_element_type=jnp.float32
            )
            summed = term if summed is None else summed + term
        return summed

    up, down = sends(me, x_ref)
    pl.when(me < n - 1)(up.start)
    pl.when(me > 0)(down.start)
    total[...] = expert_sum(x_ref[...], gates_ref[me])

    @pl.loop(1, n)
    def _(k):
        low, high = me - k, me + k

        @pl.when(low >= 0)
        def _():
            up, _ = sends(low, held.at[low])
            up.wait_recv()
            pl.when(me < n - 1)(up.start)

        @pl.when(high < n)
        def _():
            _, down = sends(high, held.at[high])
            down.wait_recv()
            pl.when(me > 0)(down.start)

        @pl.loop(0, 2)
        def _(side):
            s = me + (2 * side - 1) * k

            @pl.when((s >= 0) & (s < n))
            def _():
                parts[s] = expert_sum(held[s], gates_ref[s]).astype(jnp.bfloat16)
                copy_to(
                    parts.at[s], back.at[me], ret_sem.at[s], back_sem.at[me], exp=s
                ).start()

    @pl.loop(1, n)
    def _(k):
        f = lax.rem(me + k, n)
        copy_to(parts.at[f], back.at[f], ret_sem.at[f], back_sem.at[f], exp=f).wait_recv()
        total[...] += back[f].astype(jnp.float32)

    out_ref[...] = total[...].astype(out_ref.dtype)

    @pl.loop(1, n)
    def _(k):
        f = lax.rem(me + k, n)
        copy_to(parts.at[f], back.at[f], ret_sem.at[f], back_sem.at[f], exp=f).wait_send()

    @pl.loop(0, n)
    def _(s):
        up, down = sends(s, held.at[s])
        pl.when((s <= me) & (me < n - 1))(up.wait_send)
        pl.when((s >= me) & (me > 0))(down.wait_send)


def run_experts(expert_in, gates, switch, widen, shrink):
    n = lax.axis_size("exp")
    rows, width = expert_in.shape
    vmem = pl.BlockSpec(memory_space=pltpu.VMEM)
    return pl.pallas_call(
        functools.partial(experts_kernel, n),
        out_shape=jax.ShapeDtypeStruct((rows, width), jnp.bfloat16),
        in_specs=[vmem] * 5,
        out_specs=vmem,
        scratch_shapes=[
            pltpu.VMEM((n, rows, width), jnp.bfloat16),
            pltpu.VMEM((n, rows, width), jnp.bfloat16),
            pltpu.VMEM((n, rows, width), jnp.bfloat16),
            pltpu.VMEM((rows, width), jnp.float32),
        ]
        + [pltpu.SemaphoreType.DMA((n,))] * 5,
        compiler_params=pltpu.CompilerParams(
            collective_id=2, has_side_effects=True, vmem_limit_bytes=40 * 2**20
        ),
    )(expert_in, gates, switch, widen, shrink)


def body(
    residual_deposit_sequence,
    premix_rescaler,
    asking_projector,
    lookup_projector,
    content_projector,
    final_projector,
    logit_multipliers,
    premixture_rescaler,
    specialist_switch_tensor,
    specialist_widen_tensor,
    specialist_shrink_tensor,
    picked_specialist_labels,
    specialist_shares,
):
    specialist_slot = lax.axis_index("exp")
    exp_count = lax.axis_size("exp")
    query_heads, pairs = project_hits(
        residual_deposit_sequence[0],
        premix_rescaler,
        asking_projector,
        lookup_projector,
        content_projector,
    )
    local_lane_count = asking_projector.shape[1] // PER_LANE_DIM
    device_scratch = lax.dynamic_slice_in_dim(
        logit_multipliers, specialist_slot * local_lane_count, local_lane_count
    )
    partial_out = attend_hits(
        query_heads,
        pairs,
        final_projector,
        device_scratch,
    )
    attention_full = lax.psum_scatter(
        partial_out.astype(jnp.bfloat16), "exp", scatter_dimension=0, tiled=True
    ).astype(jnp.float32)
    attention_update = attention_full.astype(jnp.bfloat16)
    residual = residual_deposit_sequence.astype(jnp.float32) + attention_full
    expert_in = norm_rows(residual, premixture_rescaler).astype(jnp.bfloat16)
    local_experts = specialist_switch_tensor.shape[0]
    expert_ids = specialist_slot * local_experts + jnp.arange(local_experts, dtype=jnp.int32)
    gates = gates_of(picked_specialist_labels, specialist_shares, expert_ids)
    expert_update = run_experts(
        expert_in[0],
        gates,
        specialist_switch_tensor,
        specialist_widen_tensor,
        specialist_shrink_tensor,
    )[None]
    return (attention_update, expert_update)


def solution(mesh):
    placed = (
        P("exp", "blk", None),
        P(),
        P(None, "exp"),
        P(None, "exp"),
        P(None, "exp"),
        P("exp", None),
        P(),
        P(),
        P("exp", None, None),
        P("exp", None, None),
        P("exp", None, None),
        P(None, "blk", None),
        P(None, "blk", None),
    )
    return jax.shard_map(
        body,
        mesh=mesh,
        in_specs=placed,
        out_specs=(P("exp", "blk", None), P("exp", "blk", None)),
        check_vma=False,
    )
```

```python
import functools
import math

import jax
import jax.numpy as jnp
from jax import lax
from jax.experimental import pallas as pl
from jax.experimental.pallas import tpu as pltpu
from jax.sharding import PartitionSpec as P

D = 1536
PER_LANE_DIM = 128
TOP = 2
CAP = 64


def norm_rows(values, norm_gain):
    widened = values.astype(jnp.float32)
    return (
        widened * lax.rsqrt(jnp.mean(widened * widened, axis=-1, keepdims=True) + 1e-05) * norm_gain
    )


def head_norm(values):
    return values * lax.rsqrt(jnp.mean(values * values, axis=-1, keepdims=True) + 1e-06)


def attend_hits(query_heads, pairs, final_projector, logit_multipliers):
    events, row_count, _ = query_heads.shape
    lanes = logit_multipliers.shape[0]
    query_heads = query_heads.reshape(events, row_count, lanes, PER_LANE_DIM)
    pairs = jnp.swapaxes(pairs, 0, 1).reshape(events, -1, 2 * PER_LANE_DIM)
    keys, values = pairs[..., :PER_LANE_DIM], pairs[..., PER_LANE_DIM:]
    scale = logit_multipliers / math.sqrt(PER_LANE_DIM)
    scores = jnp.einsum("sigd,sjd->sgij", query_heads, keys, preferred_element_type=jnp.float32)
    expo = jnp.exp(scores * scale[None, :, None, None])
    totals = jnp.sum(expo, axis=-1)
    mixture = jnp.einsum(
        "sgij,sjd->sgid", expo.astype(jnp.bfloat16), values, preferred_element_type=jnp.float32
    )
    heads_out = head_norm(mixture / totals[..., None]).astype(jnp.bfloat16)
    out_blocks = final_projector.reshape(lanes, PER_LANE_DIM, final_projector.shape[1])
    return jnp.einsum("sgid,gde->sie", heads_out, out_blocks, preferred_element_type=jnp.float32)


def gates_of(labels, shares, expert_ids):
    hit = labels[..., None, :] == expert_ids[:, None]
    return jnp.sum(jnp.where(hit, shares[..., None, :], 0.0), axis=-1)


def greet_all(n, axis):
    me = lax.axis_index(axis)
    barrier = pltpu.get_barrier_semaphore()

    @pl.loop(1, n)
    def _(k):
        pl.semaphore_signal(
            barrier,
            inc=1,
            device_id={axis: lax.rem(me + k, n)},
            device_id_type=pl.DeviceIdType.MESH,
        )

    pl.semaphore_wait(barrier, n - 1)


def copy_to(src, dst, send_sem, recv_sem, **where):
    return pltpu.make_async_remote_copy(
        src_ref=src,
        dst_ref=dst,
        send_sem=send_sem,
        recv_sem=recv_sem,
        device_id=where,
        device_id_type=pl.DeviceIdType.MESH,
    )


def line_sends(n, me, s, block, held, up_sem, down_sem, recv_sem):
    up = copy_to(block, held.at[s], up_sem.at[s], recv_sem.at[s], exp=lax.rem(me + 1, n))
    down = copy_to(block, held.at[s], down_sem.at[s], recv_sem.at[s], exp=lax.rem(me + n - 1, n))
    return up, down


def loads(pairs, load_sem):
    return [
        pltpu.make_async_copy(source, slot, load_sem.at[i])
        for i, (source, slot) in enumerate(pairs)
    ]


def greet_both(n, blk_count):
    me, here = lax.axis_index("exp"), lax.axis_index("blk")
    barrier = pltpu.get_barrier_semaphore()

    @pl.loop(1, n)
    def _(k):
        pl.semaphore_signal(
            barrier,
            inc=1,
            device_id={"exp": lax.rem(me + k, n)},
            device_id_type=pl.DeviceIdType.MESH,
        )

    @pl.loop(1, blk_count)
    def _(k):
        pl.semaphore_signal(
            barrier,
            inc=1,
            device_id={"blk": lax.rem(here + k, blk_count)},
            device_id_type=pl.DeviceIdType.MESH,
        )

    pl.semaphore_wait(barrier, n + blk_count - 2)


def project_kernel(
    n, blk_count, x_ref, gain, asking_in, lookup_in, content_in, q_ref, kv_ref,
    asking, lookup, content, load_sem, held, up_sem, down_sem, recv_sem, kv_send_sem, kv_recv_sem,
):
    me, here = lax.axis_index("exp"), lax.axis_index("blk")
    weights = loads(
        ((lookup_in, lookup), (content_in, content), (asking_in, asking)), load_sem
    )
    for copy in weights:
        copy.start()
    greet_both(n, blk_count)

    def sends(s, block):
        return line_sends(n, me, s, block, held, up_sem, down_sem, recv_sem)

    def kv_copy(s, owner, peer):
        block = kv_ref.at[owner, s]
        return copy_to(block, block, kv_send_sem.at[s, peer], kv_recv_sem.at[s, owner], blk=peer)

    def project(s, block):
        rows = norm_rows(block, gain[...]).astype(jnp.bfloat16)
        keys = jnp.dot(rows, lookup[...], preferred_element_type=jnp.float32)
        kv_ref[here, s, :, :PER_LANE_DIM] = head_norm(keys).astype(jnp.bfloat16)
        values = jnp.dot(rows, content[...], preferred_element_type=jnp.float32)
        kv_ref[here, s, :, PER_LANE_DIM:] = values.astype(jnp.bfloat16)

        @pl.loop(1, blk_count)
        def _(k):
            kv_copy(s, here, lax.rem(here + k, blk_count)).start()

        queries = jnp.dot(rows, asking[...], preferred_element_type=jnp.float32)
        for h in range(asking.shape[1] // PER_LANE_DIM):
            lane = slice(h * PER_LANE_DIM, (h + 1) * PER_LANE_DIM)
            q_ref[s, :, lane] = head_norm(queries[:, lane]).astype(jnp.bfloat16)

    up, down = sends(me, x_ref)
    pl.when(me < n - 1)(up.start)
    pl.when(me > 0)(down.start)
    for copy in weights:
        copy.wait()
    project(me, x_ref[...])

    @pl.loop(1, n)
    def _(k):
        low, high = me - k, me + k

        @pl.when(low >= 0)
        def _():
            up, _ = sends(low, held.at[low])
            up.wait_recv()
            pl.when(me < n - 1)(up.start)

        @pl.when(high < n)
        def _():
            _, down = sends(high, held.at[high])
            down.wait_recv()
            pl.when(me > 0)(down.start)

        @pl.loop(0, 2)
        def _(side):
            s = me + (2 * side - 1) * k

            @pl.when((s >= 0) & (s < n))
            def _():
                project(s, held[s])

    @pl.loop(0, n)
    def _(s):
        up, down = sends(s, held.at[s])
        pl.when((s <= me) & (me < n - 1))(up.wait_send)
        pl.when((s >= me) & (me > 0))(down.wait_send)

        @pl.loop(1, blk_count)
        def _(k):
            peer = lax.rem(here + k, blk_count)
            kv_copy(s, here, peer).wait_send()
            kv_copy(s, peer, peer).wait_recv()


def project_hits(rows, gain, asking, lookup, content):
    n, blk_count = lax.axis_size("exp"), lax.axis_size("blk")
    count, width = rows.shape
    vmem = pl.BlockSpec(memory_space=pltpu.VMEM)
    return pl.pallas_call(
        functools.partial(project_kernel, n, blk_count),
        out_shape=(
            jax.ShapeDtypeStruct((n, count, asking.shape[1]), jnp.bfloat16),
            jax.ShapeDtypeStruct((blk_count, n, count, 2 * PER_LANE_DIM), jnp.bfloat16),
        ),
        in_specs=[vmem] * 2 + [pl.BlockSpec(memory_space=pl.ANY)] * 3,
        out_specs=(vmem, vmem),
        scratch_shapes=[pltpu.VMEM(t.shape, t.dtype) for t in (asking, lookup, content)]
        + [pltpu.SemaphoreType.DMA((3,)), pltpu.VMEM((n, count, width), jnp.bfloat16)]
        + [pltpu.SemaphoreType.DMA((n,))] * 3
        + [pltpu.SemaphoreType.DMA((n, blk_count))] * 2,
        compiler_params=pltpu.CompilerParams(
            collective_id=1, has_side_effects=True, vmem_limit_bytes=56 * 2**20
        ),
    )(rows, gain[None], asking, lookup, content)


def experts_kernel(
    n, x_ref, gates_ref, switch_in, widen_in, shrink_in, out_ref,
    switch, widen, shrink, load_sem, held, parts, back, total, up_sem, down_sem, recv_sem, ret_sem, back_sem,
):
    me = lax.axis_index("exp")
    weights = loads(((switch_in, switch), (widen_in, widen), (shrink_in, shrink)), load_sem)
    for copy in weights:
        copy.start()
    greet_all(n, "exp")

    def sends(s, block):
        return line_sends(n, me, s, block, held, up_sem, down_sem, recv_sem)

    def expert_sum(rows, gates):
        summed = None
        for j in range(switch.shape[0]):
            gate = jnp.dot(rows, switch[j], preferred_element_type=jnp.float32)
            up = jnp.dot(rows, widen[j], preferred_element_type=jnp.float32)
            hidden = gate / (1.0 + jnp.exp(-gate)) * up * gates[:, j : j + 1]
            term = jnp.dot(
                hidden.astype(jnp.bfloat16), shrink[j], preferred_element_type=jnp.float32
            )
            summed = term if summed is None else summed + term
        return summed

    up, down = sends(me, x_ref)
    pl.when(me < n - 1)(up.start)
    pl.when(me > 0)(down.start)
    for copy in weights:
        copy.wait()
    total[...] = expert_sum(x_ref[...], gates_ref[me])

    @pl.loop(1, n)
    def _(k):
        low, high = me - k, me + k

        @pl.when(low >= 0)
        def _():
            up, _ = sends(low, held.at[low])
            up.wait_recv()
            pl.when(me < n - 1)(up.start)

        @pl.when(high < n)
        def _():
            _, down = sends(high, held.at[high])
            down.wait_recv()
            pl.when(me > 0)(down.start)

        @pl.loop(0, 2)
        def _(side):
            s = me + (2 * side - 1) * k

            @pl.when((s >= 0) & (s < n))
            def _():
                parts[s] = expert_sum(held[s], gates_ref[s]).astype(jnp.bfloat16)
                copy_to(
                    parts.at[s], back.at[me], ret_sem.at[s], back_sem.at[me], exp=s
                ).start()

    @pl.loop(1, n)
    def _(k):
        f = lax.rem(me + k, n)
        copy_to(parts.at[f], back.at[f], ret_sem.at[f], back_sem.at[f], exp=f).wait_recv()
        total[...] += back[f].astype(jnp.float32)

    out_ref[...] = total[...].astype(out_ref.dtype)

    @pl.loop(1, n)
    def _(k):
        f = lax.rem(me + k, n)
        copy_to(parts.at[f], back.at[f], ret_sem.at[f], back_sem.at[f], exp=f).wait_send()

    @pl.loop(0, n)
    def _(s):
        up, down = sends(s, held.at[s])
        pl.when((s <= me) & (me < n - 1))(up.wait_send)
        pl.when((s >= me) & (me > 0))(down.wait_send)


def run_experts(expert_in, gates, switch, widen, shrink):
    n = lax.axis_size("exp")
    rows, width = expert_in.shape
    vmem = pl.BlockSpec(memory_space=pltpu.VMEM)
    return pl.pallas_call(
        functools.partial(experts_kernel, n),
        out_shape=jax.ShapeDtypeStruct((rows, width), jnp.bfloat16),
        in_specs=[vmem] * 2 + [pl.BlockSpec(memory_space=pl.ANY)] * 3,
        out_specs=vmem,
        scratch_shapes=[pltpu.VMEM(t.shape, t.dtype) for t in (switch, widen, shrink)]
        + [
            pltpu.SemaphoreType.DMA((3,)),
            pltpu.VMEM((n, rows, width), jnp.bfloat16),
            pltpu.VMEM((n, rows, width), jnp.bfloat16),
            pltpu.VMEM((n, rows, width), jnp.bfloat16),
            pltpu.VMEM((rows, width), jnp.float32),
        ]
        + [pltpu.SemaphoreType.DMA((n,))] * 5,
        compiler_params=pltpu.CompilerParams(
            collective_id=2, has_side_effects=True, vmem_limit_bytes=56 * 2**20
        ),
    )(expert_in, gates, switch, widen, shrink)


def body(
    residual_deposit_sequence,
    premix_rescaler,
    asking_projector,
    lookup_projector,
    content_projector,
    final_projector,
    logit_multipliers,
    premixture_rescaler,
    specialist_switch_tensor,
    specialist_widen_tensor,
    specialist_shrink_tensor,
    picked_specialist_labels,
    specialist_shares,
):
    specialist_slot = lax.axis_index("exp")
    exp_count = lax.axis_size("exp")
    query_heads, pairs = project_hits(
        residual_deposit_sequence[0],
        premix_rescaler,
        asking_projector,
        lookup_projector,
        content_projector,
    )
    local_lane_count = asking_projector.shape[1] // PER_LANE_DIM
    device_scratch = lax.dynamic_slice_in_dim(
        logit_multipliers, specialist_slot * local_lane_count, local_lane_count
    )
    partial_out = attend_hits(
        query_heads,
        pairs,
        final_projector,
        device_scratch,
    )
    attention_full = lax.psum_scatter(
        partial_out.astype(jnp.bfloat16), "exp", scatter_dimension=0, tiled=True
    ).astype(jnp.float32)
    attention_update = attention_full.astype(jnp.bfloat16)
    residual = residual_deposit_sequence.astype(jnp.float32) + attention_full
    expert_in = norm_rows(residual, premixture_rescaler).astype(jnp.bfloat16)
    local_experts = specialist_switch_tensor.shape[0]
    expert_ids = specialist_slot * local_experts + jnp.arange(local_experts, dtype=jnp.int32)
    gates = gates_of(picked_specialist_labels, specialist_shares, expert_ids)
    expert_update = run_experts(
        expert_in[0],
        gates,
        specialist_switch_tensor,
        specialist_widen_tensor,
        specialist_shrink_tensor,
    )[None]
    return (attention_update, expert_update)


def solution(mesh):
    placed = (
        P("exp", "blk", None),
        P(),
        P(None, "exp"),
        P(None, "exp"),
        P(None, "exp"),
        P("exp", None),
        P(),
        P(),
        P("exp", None, None),
        P("exp", None, None),
        P("exp", None, None),
        P(None, "blk", None),
        P(None, "blk", None),
    )
    return jax.shard_map(
        body,
        mesh=mesh,
        in_specs=placed,
        out_specs=(P("exp", "blk", None), P("exp", "blk", None)),
        check_vma=False,
    )
```

```python
import functools
import math

import jax
import jax.numpy as jnp
from jax import lax
from jax.experimental import pallas as pl
from jax.experimental.pallas import tpu as pltpu
from jax.sharding import PartitionSpec as P

D = 1536
PER_LANE_DIM = 128
TOP = 2
CAP = 64


def norm_rows(values, norm_gain):
    widened = values.astype(jnp.float32)
    return (
        widened * lax.rsqrt(jnp.mean(widened * widened, axis=-1, keepdims=True) + 1e-05) * norm_gain
    )


def head_norm(values):
    return values * lax.rsqrt(jnp.mean(values * values, axis=-1, keepdims=True) + 1e-06)


def gates_of(labels, shares, expert_ids):
    hit = labels[..., None, :] == expert_ids[:, None]
    return jnp.sum(jnp.where(hit, shares[..., None, :], 0.0), axis=-1)


def greet_all(n, axis):
    me = lax.axis_index(axis)
    barrier = pltpu.get_barrier_semaphore()

    @pl.loop(1, n)
    def _(k):
        pl.semaphore_signal(
            barrier,
            inc=1,
            device_id={axis: lax.rem(me + k, n)},
            device_id_type=pl.DeviceIdType.MESH,
        )

    pl.semaphore_wait(barrier, n - 1)


def copy_to(src, dst, send_sem, recv_sem, **where):
    return pltpu.make_async_remote_copy(
        src_ref=src,
        dst_ref=dst,
        send_sem=send_sem,
        recv_sem=recv_sem,
        device_id=where,
        device_id_type=pl.DeviceIdType.MESH,
    )


def line_sends(n, me, s, block, held, up_sem, down_sem, recv_sem):
    up = copy_to(block, held.at[s], up_sem.at[s], recv_sem.at[s], exp=lax.rem(me + 1, n))
    down = copy_to(block, held.at[s], down_sem.at[s], recv_sem.at[s], exp=lax.rem(me + n - 1, n))
    return up, down


def loads(pairs, load_sem):
    return [
        pltpu.make_async_copy(source, slot, load_sem.at[i])
        for i, (source, slot) in enumerate(pairs)
    ]


def greet_both(n, blk_count):
    me, here = lax.axis_index("exp"), lax.axis_index("blk")
    barrier = pltpu.get_barrier_semaphore()

    @pl.loop(1, n)
    def _(k):
        pl.semaphore_signal(
            barrier,
            inc=1,
            device_id={"exp": lax.rem(me + k, n)},
            device_id_type=pl.DeviceIdType.MESH,
        )

    @pl.loop(1, blk_count)
    def _(k):
        pl.semaphore_signal(
            barrier,
            inc=1,
            device_id={"blk": lax.rem(here + k, blk_count)},
            device_id_type=pl.DeviceIdType.MESH,
        )

    pl.semaphore_wait(barrier, n + blk_count - 2)


def project_kernel(
    n, blk_count, x_ref, gain, asking_in, lookup_in, content_in, q_ref, kv_ref,
    asking, lookup, content, load_sem, held, up_sem, down_sem, recv_sem, kv_send_sem, kv_recv_sem,
):
    me, here = lax.axis_index("exp"), lax.axis_index("blk")
    weights = loads(
        ((lookup_in, lookup), (content_in, content), (asking_in, asking)), load_sem
    )
    for copy in weights:
        copy.start()
    greet_both(n, blk_count)

    def sends(s, block):
        return line_sends(n, me, s, block, held, up_sem, down_sem, recv_sem)

    def kv_copy(s, owner, peer):
        block = kv_ref.at[owner, s]
        return copy_to(block, block, kv_send_sem.at[s, peer], kv_recv_sem.at[s, owner], blk=peer)

    def project(s, block):
        rows = norm_rows(block, gain[...]).astype(jnp.bfloat16)
        keys = jnp.dot(rows, lookup[...], preferred_element_type=jnp.float32)
        kv_ref[here, s, :, :PER_LANE_DIM] = head_norm(keys).astype(jnp.bfloat16)
        values = jnp.dot(rows, content[...], preferred_element_type=jnp.float32)
        kv_ref[here, s, :, PER_LANE_DIM:] = values.astype(jnp.bfloat16)

        @pl.loop(1, blk_count)
        def _(k):
            kv_copy(s, here, lax.rem(here + k, blk_count)).start()

        queries = jnp.dot(rows, asking[...], preferred_element_type=jnp.float32)
        for h in range(asking.shape[1] // PER_LANE_DIM):
            lane = slice(h * PER_LANE_DIM, (h + 1) * PER_LANE_DIM)
            q_ref[s, :, lane] = head_norm(queries[:, lane]).astype(jnp.bfloat16)

    up, down = sends(me, x_ref)
    pl.when(me < n - 1)(up.start)
    pl.when(me > 0)(down.start)
    for copy in weights:
        copy.wait()
    project(me, x_ref[...])

    @pl.loop(1, n)
    def _(k):
        low, high = me - k, me + k

        @pl.when(low >= 0)
        def _():
            up, _ = sends(low, held.at[low])
            up.wait_recv()
            pl.when(me < n - 1)(up.start)

        @pl.when(high < n)
        def _():
            _, down = sends(high, held.at[high])
            down.wait_recv()
            pl.when(me > 0)(down.start)

        @pl.loop(0, 2)
        def _(side):
            s = me + (2 * side - 1) * k

            @pl.when((s >= 0) & (s < n))
            def _():
                project(s, held[s])

    @pl.loop(0, n)
    def _(s):
        up, down = sends(s, held.at[s])
        pl.when((s <= me) & (me < n - 1))(up.wait_send)
        pl.when((s >= me) & (me > 0))(down.wait_send)

        @pl.loop(1, blk_count)
        def _(k):
            peer = lax.rem(here + k, blk_count)
            kv_copy(s, here, peer).wait_send()
            kv_copy(s, peer, peer).wait_recv()


def project_hits(rows, gain, asking, lookup, content):
    n, blk_count = lax.axis_size("exp"), lax.axis_size("blk")
    count, width = rows.shape
    vmem = pl.BlockSpec(memory_space=pltpu.VMEM)
    return pl.pallas_call(
        functools.partial(project_kernel, n, blk_count),
        out_shape=(
            jax.ShapeDtypeStruct((n, count, asking.shape[1]), jnp.bfloat16),
            jax.ShapeDtypeStruct((blk_count, n, count, 2 * PER_LANE_DIM), jnp.bfloat16),
        ),
        in_specs=[vmem] * 2 + [pl.BlockSpec(memory_space=pl.ANY)] * 3,
        out_specs=(vmem, vmem),
        scratch_shapes=[pltpu.VMEM(t.shape, t.dtype) for t in (asking, lookup, content)]
        + [pltpu.SemaphoreType.DMA((3,)), pltpu.VMEM((n, count, width), jnp.bfloat16)]
        + [pltpu.SemaphoreType.DMA((n,))] * 3
        + [pltpu.SemaphoreType.DMA((n, blk_count))] * 2,
        compiler_params=pltpu.CompilerParams(
            collective_id=1, has_side_effects=True, vmem_limit_bytes=56 * 2**20
        ),
    )(rows, gain[None], asking, lookup, content)


def attend_kernel(
    n, q_ref, kv_ref, scale_ref, final, x_ref, gain, update_ref, expert_in_ref,
    parts, back, total, ret_sem, back_sem,
):
    me = lax.axis_index("exp")
    greet_all(n, "exp")

    def block_of(f):
        pairs = kv_ref[:, f].reshape(-1, 2 * PER_LANE_DIM)
        keys, values = pairs[:, :PER_LANE_DIM], pairs[:, PER_LANE_DIM:]
        summed = None
        for h in range(final.shape[0] // PER_LANE_DIM):
            lane = slice(h * PER_LANE_DIM, (h + 1) * PER_LANE_DIM)
            scores = lax.dot_general(
                q_ref[f, :, lane],
                keys,
                (((1,), (1,)), ((), ())),
                preferred_element_type=jnp.float32,
            )
            expo = jnp.exp(scores * scale_ref[h])
            mixture = jnp.dot(
                expo.astype(jnp.bfloat16), values, preferred_element_type=jnp.float32
            ) / jnp.sum(expo, axis=-1, keepdims=True)
            term = jnp.dot(
                head_norm(mixture).astype(jnp.bfloat16),
                final[lane, :],
                preferred_element_type=jnp.float32,
            )
            summed = term if summed is None else summed + term
        return summed

    def returned(f):
        return copy_to(parts.at[f], back.at[f], ret_sem.at[f], back_sem.at[f], exp=f)

    @pl.loop(1, n)
    def _(k):
        f = lax.rem(me + k, n)
        parts[f] = block_of(f).astype(jnp.bfloat16)
        copy_to(parts.at[f], back.at[me], ret_sem.at[f], back_sem.at[me], exp=f).start()

    total[...] = block_of(me)

    @pl.loop(1, n)
    def _(k):
        f = lax.rem(me + k, n)
        returned(f).wait_recv()
        total[...] += back[f].astype(jnp.float32)

    update_ref[...] = total[...].astype(jnp.bfloat16)
    residual = x_ref[...].astype(jnp.float32) + total[...]
    expert_in_ref[...] = norm_rows(residual, gain[...]).astype(jnp.bfloat16)

    @pl.loop(1, n)
    def _(k):
        returned(lax.rem(me + k, n)).wait_send()


def attend_hits(query_heads, pairs, logit_multipliers, final_projector, rows, gain):
    n = lax.axis_size("exp")
    vmem = pl.BlockSpec(memory_space=pltpu.VMEM)
    shape = jax.ShapeDtypeStruct(rows.shape, jnp.bfloat16)
    return pl.pallas_call(
        functools.partial(attend_kernel, n),
        out_shape=(shape, shape),
        in_specs=[vmem, vmem, pl.BlockSpec(memory_space=pltpu.SMEM), vmem, vmem, vmem],
        out_specs=(vmem, vmem),
        scratch_shapes=[
            pltpu.VMEM((n, *rows.shape), jnp.bfloat16),
            pltpu.VMEM((n, *rows.shape), jnp.bfloat16),
            pltpu.VMEM(rows.shape, jnp.float32),
        ]
        + [pltpu.SemaphoreType.DMA((n,))] * 2,
        compiler_params=pltpu.CompilerParams(
            collective_id=3, has_side_effects=True, vmem_limit_bytes=56 * 2**20
        ),
    )(
        query_heads,
        pairs,
        logit_multipliers / math.sqrt(PER_LANE_DIM),
        final_projector,
        rows,
        gain[None],
    )


def experts_kernel(
    n, x_ref, gates_ref, switch_in, widen_in, shrink_in, out_ref,
    switch, widen, shrink, load_sem, held, parts, back, total, up_sem, down_sem, recv_sem, ret_sem, back_sem,
):
    me = lax.axis_index("exp")
    weights = loads(((switch_in, switch), (widen_in, widen), (shrink_in, shrink)), load_sem)
    for copy in weights:
        copy.start()
    greet_all(n, "exp")

    def sends(s, block):
        return line_sends(n, me, s, block, held, up_sem, down_sem, recv_sem)

    def expert_sum(rows, gates):
        summed = None
        for j in range(switch.shape[0]):
            gate = jnp.dot(rows, switch[j], preferred_element_type=jnp.float32)
            up = jnp.dot(rows, widen[j], preferred_element_type=jnp.float32)
            hidden = gate / (1.0 + jnp.exp(-gate)) * up * gates[:, j : j + 1]
            term = jnp.dot(
                hidden.astype(jnp.bfloat16), shrink[j], preferred_element_type=jnp.float32
            )
            summed = term if summed is None else summed + term
        return summed

    up, down = sends(me, x_ref)
    pl.when(me < n - 1)(up.start)
    pl.when(me > 0)(down.start)
    for copy in weights:
        copy.wait()
    total[...] = expert_sum(x_ref[...], gates_ref[me])

    @pl.loop(1, n)
    def _(k):
        low, high = me - k, me + k

        @pl.when(low >= 0)
        def _():
            up, _ = sends(low, held.at[low])
            up.wait_recv()
            pl.when(me < n - 1)(up.start)

        @pl.when(high < n)
        def _():
            _, down = sends(high, held.at[high])
            down.wait_recv()
            pl.when(me > 0)(down.start)

        @pl.loop(0, 2)
        def _(side):
            s = me + (2 * side - 1) * k

            @pl.when((s >= 0) & (s < n))
            def _():
                parts[s] = expert_sum(held[s], gates_ref[s]).astype(jnp.bfloat16)
                copy_to(
                    parts.at[s], back.at[me], ret_sem.at[s], back_sem.at[me], exp=s
                ).start()

    @pl.loop(1, n)
    def _(k):
        f = lax.rem(me + k, n)
        copy_to(parts.at[f], back.at[f], ret_sem.at[f], back_sem.at[f], exp=f).wait_recv()
        total[...] += back[f].astype(jnp.float32)

    out_ref[...] = total[...].astype(out_ref.dtype)

    @pl.loop(1, n)
    def _(k):
        f = lax.rem(me + k, n)
        copy_to(parts.at[f], back.at[f], ret_sem.at[f], back_sem.at[f], exp=f).wait_send()

    @pl.loop(0, n)
    def _(s):
        up, down = sends(s, held.at[s])
        pl.when((s <= me) & (me < n - 1))(up.wait_send)
        pl.when((s >= me) & (me > 0))(down.wait_send)


def run_experts(expert_in, gates, switch, widen, shrink):
    n = lax.axis_size("exp")
    rows, width = expert_in.shape
    vmem = pl.BlockSpec(memory_space=pltpu.VMEM)
    return pl.pallas_call(
        functools.partial(experts_kernel, n),
        out_shape=jax.ShapeDtypeStruct((rows, width), jnp.bfloat16),
        in_specs=[vmem] * 2 + [pl.BlockSpec(memory_space=pl.ANY)] * 3,
        out_specs=vmem,
        scratch_shapes=[pltpu.VMEM(t.shape, t.dtype) for t in (switch, widen, shrink)]
        + [
            pltpu.SemaphoreType.DMA((3,)),
            pltpu.VMEM((n, rows, width), jnp.bfloat16),
            pltpu.VMEM((n, rows, width), jnp.bfloat16),
            pltpu.VMEM((n, rows, width), jnp.bfloat16),
            pltpu.VMEM((rows, width), jnp.float32),
        ]
        + [pltpu.SemaphoreType.DMA((n,))] * 5,
        compiler_params=pltpu.CompilerParams(
            collective_id=2, has_side_effects=True, vmem_limit_bytes=56 * 2**20
        ),
    )(expert_in, gates, switch, widen, shrink)


def body(
    residual_deposit_sequence,
    premix_rescaler,
    asking_projector,
    lookup_projector,
    content_projector,
    final_projector,
    logit_multipliers,
    premixture_rescaler,
    specialist_switch_tensor,
    specialist_widen_tensor,
    specialist_shrink_tensor,
    picked_specialist_labels,
    specialist_shares,
):
    specialist_slot = lax.axis_index("exp")
    exp_count = lax.axis_size("exp")
    query_heads, pairs = project_hits(
        residual_deposit_sequence[0],
        premix_rescaler,
        asking_projector,
        lookup_projector,
        content_projector,
    )
    local_lane_count = asking_projector.shape[1] // PER_LANE_DIM
    device_scratch = lax.dynamic_slice_in_dim(
        logit_multipliers, specialist_slot * local_lane_count, local_lane_count
    )
    attention_update, expert_in = attend_hits(
        query_heads,
        pairs,
        device_scratch,
        final_projector,
        residual_deposit_sequence[0],
        premixture_rescaler,
    )
    local_experts = specialist_switch_tensor.shape[0]
    expert_ids = specialist_slot * local_experts + jnp.arange(local_experts, dtype=jnp.int32)
    gates = gates_of(picked_specialist_labels, specialist_shares, expert_ids)
    expert_update = run_experts(
        expert_in,
        gates,
        specialist_switch_tensor,
        specialist_widen_tensor,
        specialist_shrink_tensor,
    )[None]
    return (attention_update[None], expert_update)


def solution(mesh):
    placed = (
        P("exp", "blk", None),
        P(),
        P(None, "exp"),
        P(None, "exp"),
        P(None, "exp"),
        P("exp", None),
        P(),
        P(),
        P("exp", None, None),
        P("exp", None, None),
        P("exp", None, None),
        P(None, "blk", None),
        P(None, "blk", None),
    )
    return jax.shard_map(
        body,
        mesh=mesh,
        in_specs=placed,
        out_specs=(P("exp", "blk", None), P("exp", "blk", None)),
        check_vma=False,
    )
```
